512 devices in a mesh: row: 8 (over z), col: 16 (over y_hi, x, core), kpart: 4 (over y_lo).
Axes of the slice: x: 4, y: 8 (y_hi: 2, y_lo: 4; y = y_hi * 4 + y_lo), z: 8, core: 2. Of those that a mesh axis runs over, the one named last changes fastest.
Arguments:
- left_cyclic: float32 [2048, 8192], P(('kpart', 'col'), 'row'), may hold values from -6 to 6
- right_cyclic: float32 [2048, 16384], P(('kpart', 'row'), 'col'), may hold values from -0.125 to 0.125
Outputs:
- product: float32 [8192, 16384], P(('row', 'kpart'), 'col')
The draws below stay inside these ranges and needn't reach their ends.
All inputs are finite; a program needn't handle non-finite values.
Results may differ from the reference program's by a relative error of at most 0.00007.
Values sent between devices are 32-bit elements; how exact they have to be, the bound alone decides.
No kernel may reach another device: no remote copies, remote signals or barrier semaphores. Data moves between devices by JAX's collectives and lax.ppermute only.
A program may use at most 64 MiB of HBM per device.

```python
import jax
import jax.numpy as jnp
from jax import lax

M = 8192
N = 16384
K = 2048
NB = 64
N_ROW = 8
N_COL = 16


def levels(own_key, extent, pieces, least, top_value):
    def one(position, blocks):
        heights = jax.random.uniform(jax.random.fold_in(jax.random.fold_in(own_key, 6), position), (blocks,), jnp.float32, least / len(pieces), top_value / len(pieces))
        return jnp.repeat(jnp.exp(heights), extent[position] // blocks).reshape((-1,) + (1,) * (len(extent) - position - 1))

    factor_of = one(*pieces[0])
    for cut in pieces[1:]:
        factor_of = factor_of * one(*cut)
    return factor_of


def scatter_about(stream_key, dims, scale, most, pieces=(), dtype=jnp.bfloat16):
    level = levels(stream_key, dims, pieces, -0.22, 0.18) if pieces else 1.0
    array = jax.random.normal(stream_key, dims, jnp.float32) * scale * level
    return jnp.minimum(jnp.maximum(array, -most), most).astype(dtype)


def setup_inputs(seed: int = 0) -> dict:
    seeds = jax.random.split(jax.random.key(seed), 3)
    left_cyclic = scatter_about(seeds[0], (K, M), 1.0, 6.0, ((0, 64), (1, 8)), jnp.float32)
    right_cyclic = scatter_about(seeds[1], (K, N), K ** -0.5, 0.125, ((0, 32), (1, 16)), jnp.float32)
    return dict(left_cyclic=left_cyclic, right_cyclic=right_cyclic)


def reference(left_cyclic, right_cyclic):
    left_global = left_cyclic.reshape(K, N_ROW, M // (N_ROW * NB), NB)
    left_global = left_global.transpose(0, 2, 1, 3).reshape(K, M)
    right_global = right_cyclic.reshape(K, N_COL, N // (N_COL * NB), NB)
    right_global = right_global.transpose(0, 2, 1, 3).reshape(K, N)
    return lax.dot_general(left_global, right_global, (((0,), (0,)), ((), ())), precision=lax.Precision.HIGHEST, preferred_element_type=jnp.float32)
```

```python
import functools

import jax
import jax.numpy as jnp
from jax import lax
from jax.experimental import pallas as pl
from jax.experimental.pallas import tpu as pltpu
from jax.sharding import Mesh, PartitionSpec as P

F32 = jnp.float32
BF16 = jnp.bfloat16
PLACE = ((0, 2, 1, 3), (1, 3, 2, 0))


def whole(n):
    return [pl.BlockSpec(memory_space=pltpu.VMEM)] * n


def params():
    return pltpu.CompilerParams(vmem_limit_bytes=24 * 1024 * 1024)


def groups(shape, width):
    return lax.broadcasted_iota(jnp.int32, shape, len(shape) - 1) // width


def pick(where, parts):
    out = parts[0]
    for g in range(1, len(parts)):
        out = jnp.where(where == g, parts[g], out)
    return out


def pack_right_kernel(x_ref, out_ref):
    g = groups((16, 128), 32)
    for hx in range(8):
        rolled = []
        for i in range(4):
            tile = x_ref[16 * i : 16 * i + 16, 128 * hx : 128 * hx + 128]
            rolled.append(pltpu.roll(tile, 32 * i, 1) if i else tile)
        for p in range(4):
            msg = pick(g, [rolled[(k - p) % 4] for k in range(4)])
            for a in range(2):
                out_ref[(2 * hx + p // 2) * 4 + 2 * a + p % 2] = msg


def unpack_right_kernel(core, half, in_ref, out_ref):
    g = groups((16, 128), 32)
    core, half = core(), half()
    p = 2 * core + half

    def run(place):
        for l in range(4):
            for t in range(4):
                rolled = []
                for m in range(4):
                    msg = in_ref[(4 * t + m) * 4 + l]
                    rolled.append(pltpu.roll(msg, 32 * place[m], 1) if place[m] else msg)
                for j in range(4):
                    order = [None] * 4
                    for m in range(4):
                        order[(j + place[m]) % 4] = rolled[m]
                    row = pick(g, order)
                    if j:
                        row = pltpu.roll(row, 32 * (4 - j), 1)
                    i = lax.rem(j - p + 4, 4)
                    s = i // 2
                    out_ref[lax.rem(s + core, 2), l, lax.rem(i, 2), :, 128 * t : 128 * t + 128] = row

    for h in range(2):
        pl.when(half == h)(functools.partial(run, PLACE[h]))


def pack_left_kernel(x_ref, out_ref):
    low = groups((16, 128), 64) == 0
    for z in range(8):
        top = x_ref[0:16, 128 * z : 128 * z + 128]
        bottom = x_ref[16:32, 128 * z : 128 * z + 128]
        first = jnp.where(low, top, pltpu.roll(bottom, 64, 1))
        second = jnp.where(low, pltpu.roll(top, 64, 1), bottom)
        for h in range(2):
            for b in range(2):
                out_ref[z * 8 + h * 4 + b] = first
                out_ref[z * 8 + h * 4 + 2 + b] = second


def unpack_left_kernel(in_ref, *refs):
    out_ref = refs[-1]
    low = groups((16, 128), 64) == 0
    for h in range(2):
        for t in range(4):
            rows = []
            for l in range(4):
                even = in_ref[(2 * t) * 8 + h * 4 + l]
                odd = in_ref[(2 * t + 1) * 8 + h * 4 + l]
                rows.append(jnp.where(low, even, pltpu.roll(odd, 64, 1)))
                rows.append(jnp.where(low, pltpu.roll(even, 64, 1), odd))
            block = jnp.concatenate(rows, axis=0).T
            for d in range(4):
                out_ref[d, h, 128 * t : 128 * t + 128, :] = block


def split(x):
    high = x.astype(BF16)
    return high, (x - high.astype(F32)).astype(BF16)


def product(left, right):
    a, c = split(left)
    b, d = split(right)
    dot = functools.partial(jnp.dot, preferred_element_type=F32)
    return dot(a, b) + dot(a, d) + dot(c, b)


def term_kernel(sizes, first, *refs):
    refs = list(refs[1:])
    acc = None if first else refs[-2][...]
    for size in sizes:
        own, other = refs.pop(0), refs.pop(0)
        parts = [refs.pop(0)[...].reshape(256 // size, 512) for _ in range(size)]
        a = jnp.concatenate([own[0], other[0]], axis=1)
        x = product(a, jnp.concatenate(parts, axis=0) if size > 1 else parts[0])
        acc = x if acc is None else acc + x
    refs[-1][...] = acc


def terms(at, own, other, chunks, acc, tiles):
    one = tiles == 1
    tile = (lambda m, at: at[0]) if one else (lambda m, at: m)
    specs, ops = [], []
    for k, chunk in enumerate(chunks):
        left = pl.BlockSpec((1, 256, 128), functools.partial(lambda k, m, at: (at[k + 1], tile(m, at), 0), k))
        specs += [left, left]
        ops += [own, other]
        for part in chunk:
            specs.append(pl.BlockSpec(part.shape, lambda m, at: (0, 0, 0)))
            ops.append(part)
    if acc is not None:
        specs.append(pl.BlockSpec((256, 512), lambda m, at: (tile(m, at), 0)))
        ops.append(acc)
    return pl.pallas_call(
        functools.partial(term_kernel, [len(c) for c in chunks], acc is None),
        grid_spec=pltpu.PrefetchScalarGridSpec(
            num_scalar_prefetch=1,
            grid=(tiles,),
            in_specs=specs,
            out_specs=pl.BlockSpec((256, 512), lambda m, at: (m, 0)),
        ),
        out_shape=jax.ShapeDtypeStruct((256 * tiles, 512), F32),
        compiler_params=params(),
        cost_estimate=pl.CostEstimate(
            flops=6 * 256 * len(chunks) * 512 * 256 * tiles, bytes_accessed=4 * 512 * 512, transcendentals=0
        ),
    )(at, *ops)


def finish_kernel(half, mine_ref, got_ref, out_ref):
    own = (groups((256, 128), 32) % 2) == half()
    for t in range(4):
        mine = mine_ref[:, 128 * t : 128 * t + 128]
        got = got_ref[:, 128 * t : 128 * t + 128]
        out_ref[:, 256 * t : 256 * t + 128] = jnp.where(own, mine, got)
        out_ref[:, 256 * t + 128 : 256 * t + 256] = pltpu.roll(jnp.where(own, got, mine), 96, 1)


def shift(x, axis, by, n):
    return lax.ppermute(x, axis, [(i, (i + by) % n) for i in range(n)])


def core_index():
    return lax.axis_index("c")


def half_index():
    return lax.rem(lax.axis_index("l"), 2)


def call(kernel, shape, *ops, specs=None):
    return pl.pallas_call(
        kernel,
        in_specs=specs or whole(len(ops)),
        out_specs=pl.BlockSpec(memory_space=pltpu.VMEM),
        out_shape=jax.ShapeDtypeStruct(shape, F32),
        compiler_params=params(),
    )(*ops)


def shards(left, right):
    z = lax.axis_index("z")
    b = half_index()
    r = call(pack_right_kernel, (64, 16, 128), right)
    q = call(pack_left_kernel, (64, 16, 128), left)
    r = lax.all_to_all(r, ("h", "x", "c", "l"), 0, 0, tiled=True)
    r = call(functools.partial(unpack_right_kernel, core_index, half_index), (2, 4, 2, 16, 512), r)
    r = r.reshape(2, 128, 512)

    q, r = lax.optimization_barrier((q, r))
    up1, down1 = shift(r, "z", 1, 8), shift(r, "z", -1, 8)
    q = lax.all_to_all(q, ("z", "h", "l"), 0, 0, tiled=True)
    q, up1, down1 = lax.optimization_barrier((q, up1, down1))
    up2, down2 = shift(up1, "z", 1, 8), shift(down1, "z", -1, 8)
    q = call(unpack_left_kernel, (4, 2, 512, 128), q)
    own = lax.all_to_all(q, "x", 0, 0, tiled=True).reshape(8, 512, 128)
    own, up2, down2 = lax.optimization_barrier((own, up2, down2))
    other = lax.ppermute(own, "c", [(0, 1), (1, 0)])
    up3, down3 = shift(up2, "z", 1, 8), shift(down2, "z", -1, 8)
    other, up3, down3 = lax.optimization_barrier((other, up3, down3))

    def at(tile, *steps):
        zs = (z + jnp.array(steps)) % 8
        return jnp.concatenate([jnp.full((1,), tile, jnp.int32), (zs % 4) * 2 + zs // 4]).astype(jnp.int32)

    total = terms(at(0, 0, -1, 1), own, other, [(r,), (up1,), (down1,)], None, 2)
    total = terms(at(0, -2, 2), own, other, [(up2,), (down2,)], total, 2)
    total = terms(at(0, -3, 3), own, other, [(up3,), (down3,)], total, 2)
    up4 = shift(up3[:1], "z", 1, 8)
    down4 = shift(down3[1:], "z", -1, 8)
    total, up4, down4 = lax.optimization_barrier((total, up4, down4))
    last = (up4, down4)
    theirs = terms(at(1 - b, 4), own, other, [last], total, 1)
    got = lax.ppermute(theirs, "l", [(0, 1), (1, 0), (2, 3), (3, 2)])
    mine = terms(at(b, 4), own, other, [last], total, 1)
    return call(functools.partial(finish_kernel, half_index), (256, 1024), mine, got)


def solution(mesh):
    fine = Mesh(mesh.devices.reshape(8, 2, 4, 2, 4), ("z", "h", "x", "c", "l"))
    col = ("h", "x", "c")
    return jax.shard_map(
        shards,
        mesh=fine,
        in_specs=(P(("l",) + col, "z"), P(("l", "z"), col)),
        out_specs=P(("z", "l"), col),
        check_vma=False,
    )
```

```python
import functools

import jax
import jax.numpy as jnp
from jax import lax
from jax.experimental import pallas as pl
from jax.experimental.pallas import tpu as pltpu
from jax.sharding import Mesh, PartitionSpec as P

F32 = jnp.float32
BF16 = jnp.bfloat16
PLACE = ((0, 2, 1, 3), (1, 3, 2, 0))


def params():
    return pltpu.CompilerParams(vmem_limit_bytes=8 * 1024 * 1024)


def groups(shape, width):
    return lax.broadcasted_iota(jnp.int32, shape, len(shape) - 1) // width


def pick(where, parts):
    out = parts[0]
    for g in range(1, len(parts)):
        out = jnp.where(where == g, parts[g], out)
    return out


def pack_right_kernel(x_ref, out_ref):
    g = groups((16, 128), 32)
    for hx in range(8):
        rolled = []
        for i in range(4):
            tile = x_ref[16 * i : 16 * i + 16, 128 * hx : 128 * hx + 128]
            rolled.append(pltpu.roll(tile, 32 * i, 1) if i else tile)
        for p in range(4):
            msg = pick(g, [rolled[(k - p) % 4] for k in range(4)])
            for a in range(2):
                out_ref[(2 * hx + p // 2) * 4 + 2 * a + p % 2] = msg


def unpack_right_kernel(core, half, in_ref, out_ref):
    g = groups((16, 128), 32)
    core, half = core(), half()
    p = 2 * core + half

    def run(place):
        for l in range(4):
            for t in range(4):
                rolled = []
                for m in range(4):
                    msg = in_ref[(4 * t + m) * 4 + l]
                    rolled.append(pltpu.roll(msg, 32 * place[m], 1) if place[m] else msg)
                for j in range(4):
                    order = [None] * 4
                    for m in range(4):
                        order[(j + place[m]) % 4] = rolled[m]
                    row = pick(g, order)
                    if j:
                        row = pltpu.roll(row, 32 * (4 - j), 1)
                    i = lax.rem(j - p + 4, 4)
                    s = i // 2
                    out_ref[lax.rem(s + core, 2), l, lax.rem(i, 2), :, 128 * t : 128 * t + 128] = row

    for h in range(2):
        pl.when(half == h)(functools.partial(run, PLACE[h]))


def pack_left_kernel(x_ref, out_ref):
    low = groups((16, 128), 64) == 0
    for z in range(8):
        top = x_ref[0:16, 128 * z : 128 * z + 128]
        bottom = x_ref[16:32, 128 * z : 128 * z + 128]
        first = jnp.where(low, top, pltpu.roll(bottom, 64, 1))
        second = jnp.where(low, pltpu.roll(top, 64, 1), bottom)
        for h in range(2):
            for b in range(2):
                out_ref[z * 8 + h * 4 + b] = first
                out_ref[z * 8 + h * 4 + 2 + b] = second


def unpack_left_kernel(half, in_ref, theirs_ref, mine_ref):
    low = groups((16, 128), 64) == 0

    def run(outs):
        for h in range(2):
            for t in range(4):
                rows = []
                for l in range(4):
                    even = in_ref[(2 * t) * 8 + h * 4 + l]
                    odd = in_ref[(2 * t + 1) * 8 + h * 4 + l]
                    rows.append(jnp.where(low, even, pltpu.roll(odd, 64, 1)))
                    rows.append(jnp.where(low, pltpu.roll(even, 64, 1), odd))
                block = jnp.concatenate(rows, axis=0).T
                for d in range(4):
                    outs[t // 2][d, h, t % 2 * 128 : t % 2 * 128 + 128, :] = block

    half = half()
    pl.when(half == 0)(functools.partial(run, (mine_ref, theirs_ref)))
    pl.when(half == 1)(functools.partial(run, (theirs_ref, mine_ref)))


def split(x):
    high = x.astype(BF16)
    return high, (x - high.astype(F32)).astype(BF16)


def product(left, right):
    a, c = split(left)
    b, d = split(right)
    dot = functools.partial(jnp.dot, preferred_element_type=F32)
    return dot(a, b) + dot(a, d) + dot(c, b)


def terms_kernel(own_ref, other_ref, right_ref, out_ref, left, right, sems):
    copies = []
    for z in range(8):
        at = z % 4 * 2 + z // 4
        copies.append(
            [
                pltpu.make_async_copy(own_ref.at[at], left.at[z, 0], sems.at[z, 0]),
                pltpu.make_async_copy(other_ref.at[at], left.at[z, 1], sems.at[z, 1]),
                pltpu.make_async_copy(right_ref.at[z], right.at[z], sems.at[z, 2]),
            ]
        )
    for group in copies:
        for copy in group:
            copy.start()
    total = None
    for z, group in enumerate(copies):
        for copy in group:
            copy.wait()
        x = product(jnp.concatenate([left[z, 0], left[z, 1]], axis=1), right[z].reshape(256, 512))
        total = x if total is None else total + x
    out_ref[...] = total


def terms(own, other, right):
    far = pl.BlockSpec(memory_space=pl.ANY)
    return pl.pallas_call(
        terms_kernel,
        in_specs=[far] * 3,
        out_specs=pl.BlockSpec(memory_space=pltpu.VMEM),
        out_shape=jax.ShapeDtypeStruct((256, 512), F32),
        scratch_shapes=[
            pltpu.VMEM((8, 2, 256, 128), F32),
            pltpu.VMEM((8, 2, 128, 512), F32),
            pltpu.SemaphoreType.DMA((8, 3)),
        ],
        compiler_params=pltpu.CompilerParams(vmem_limit_bytes=60 * 1024 * 1024),
        cost_estimate=pl.CostEstimate(flops=6 * 256 * 2048 * 512, bytes_accessed=6 << 20, transcendentals=0),
    )(own, other, right)


def finish_kernel(half, mine_ref, got_ref, out_ref):
    own = (groups((256, 128), 32) % 2) == half()
    for t in range(4):
        mine = mine_ref[:, 128 * t : 128 * t + 128]
        got = got_ref[:, 128 * t : 128 * t + 128]
        out_ref[:, 256 * t : 256 * t + 128] = jnp.where(own, mine, got)
        out_ref[:, 256 * t + 128 : 256 * t + 256] = pltpu.roll(jnp.where(own, got, mine), 96, 1)


def core_index():
    return lax.axis_index("c")


def half_index():
    return lax.rem(lax.axis_index("l"), 2)


def call(kernel, shape, *ops, cost=0):
    spec = pl.BlockSpec(memory_space=pltpu.VMEM)
    outs = len(shape) if isinstance(shape, list) else 0
    out = [jax.ShapeDtypeStruct(s, F32) for s in shape] if outs else jax.ShapeDtypeStruct(shape, F32)
    return pl.pallas_call(
        kernel,
        in_specs=[spec] * len(ops),
        out_specs=[spec] * outs if outs else spec,
        out_shape=out,
        compiler_params=params(),
        cost_estimate=pl.CostEstimate(flops=cost, bytes_accessed=1 << 20, transcendentals=0),
    )(*ops)


def after(x, *others):
    return lax.optimization_barrier((x, *others))[0]


def swap(x, axis, n):
    return lax.ppermute(x, axis, [(i, i ^ 1) for i in range(n)])


def shards(left, right):
    r = call(pack_right_kernel, (64, 16, 128), right)
    q = call(pack_left_kernel, (64, 16, 128), left)
    r = lax.all_to_all(r, ("h", "x", "c", "l"), 0, 0, tiled=True)
    r = call(functools.partial(unpack_right_kernel, core_index, half_index), (2, 4, 2, 16, 512), r)
    r = r.reshape(2, 128, 512)
    w = lax.all_gather(r, "z", axis=0, tiled=False)

    q = lax.all_to_all(after(q, r), ("z", "h", "l"), 0, 0, tiled=True)
    theirs, mine = call(functools.partial(unpack_left_kernel, half_index), [(4, 2, 256, 128)] * 2, q)
    own1 = lax.all_to_all(theirs, "x", 0, 0, tiled=True).reshape(8, 256, 128)
    own2 = lax.all_to_all(after(mine, own1), "x", 0, 0, tiled=True).reshape(8, 256, 128)
    other1 = swap(own1, "c", 2)

    theirs = terms(own1, other1, w)
    got = swap(theirs, "l", 4)
    other2 = swap(own2, "c", 2)
    mine = terms(own2, other2, w)
    return call(functools.partial(finish_kernel, half_index), (256, 1024), mine, got)


def solution(mesh):
    fine = Mesh(mesh.devices.reshape(8, 2, 4, 2, 4), ("z", "h", "x", "c", "l"))
    col = ("h", "x", "c")
    return jax.shard_map(
        shards,
        mesh=fine,
        in_specs=(P(("l",) + col, "z"), P(("l", "z"), col)),
        out_specs=P(("z", "l"), col),
        check_vma=False,
    )
```

```python
import functools

import jax
import jax.numpy as jnp
from jax import lax
from jax.experimental import pallas as pl
from jax.experimental.pallas import tpu as pltpu
from jax.sharding import Mesh, PartitionSpec as P

F32 = jnp.float32
BF16 = jnp.bfloat16
PLACE = ((0, 2, 1, 3), (1, 3, 2, 0))


def params(limit=8):
    return pltpu.CompilerParams(vmem_limit_bytes=limit * 1024 * 1024)


def groups(shape, width):
    return lax.broadcasted_iota(jnp.int32, shape, len(shape) - 1) // width


def pick(where, parts):
    out = parts[0]
    for g in range(1, len(parts)):
        out = jnp.where(where == g, parts[g], out)
    return out


def pack_right_kernel(x_ref, out_ref):
    g = groups((16, 128), 32)
    for hx in range(8):
        rolled = []
        for i in range(4):
            tile = x_ref[16 * i : 16 * i + 16, 128 * hx : 128 * hx + 128]
            rolled.append(pltpu.roll(tile, 32 * i, 1) if i else tile)
        for p in range(4):
            msg = pick(g, [rolled[(k - p) % 4] for k in range(4)])
            for a in range(2):
                out_ref[(2 * hx + p // 2) * 4 + 2 * a + p % 2] = msg


def unpack_right_kernel(core, half, in_ref, out_ref):
    g = groups((16, 128), 32)
    core, half = core(), half()
    p = 2 * core + half

    def run(place):
        for l in range(4):
            for t in range(4):
                rolled = []
                for m in range(4):
                    msg = in_ref[(4 * t + m) * 4 + l]
                    rolled.append(pltpu.roll(msg, 32 * place[m], 1) if place[m] else msg)
                for j in range(4):
                    order = [None] * 4
                    for m in range(4):
                        order[(j + place[m]) % 4] = rolled[m]
                    row = pick(g, order)
                    if j:
                        row = pltpu.roll(row, 32 * (4 - j), 1)
                    i = lax.rem(j - p + 4, 4)
                    s = i // 2
                    out_ref[lax.rem(s + core, 2), l, lax.rem(i, 2), :, 128 * t : 128 * t + 128] = row

    for h in range(2):
        pl.when(half == h)(functools.partial(run, PLACE[h]))


def pack_left_kernel(x_ref, out_ref):
    low = groups((16, 128), 64) == 0
    for z in range(8):
        top = x_ref[0:16, 128 * z : 128 * z + 128]
        bottom = x_ref[16:32, 128 * z : 128 * z + 128]
        first = jnp.where(low, top, pltpu.roll(bottom, 64, 1))
        second = jnp.where(low, pltpu.roll(top, 64, 1), bottom)
        for h in range(2):
            for b in range(2):
                out_ref[z * 8 + h * 4 + b] = first
                out_ref[z * 8 + h * 4 + 2 + b] = second


def unpack_left_kernel(half, in_ref, theirs_ref, mine_ref):
    low = groups((16, 128), 64) == 0

    def run(outs):
        for h in range(2):
            for t in range(4):
                rows = []
                for l in range(4):
                    even = in_ref[(2 * t) * 8 + h * 4 + l]
                    odd = in_ref[(2 * t + 1) * 8 + h * 4 + l]
                    rows.append(jnp.where(low, even, pltpu.roll(odd, 64, 1)))
                    rows.append(jnp.where(low, pltpu.roll(even, 64, 1), odd))
                block = jnp.concatenate(rows, axis=0).T
                for d in range(4):
                    outs[t // 2][d, h, t % 2 * 128 : t % 2 * 128 + 128, :] = block

    half = half()
    pl.when(half == 0)(functools.partial(run, (mine_ref, theirs_ref)))
    pl.when(half == 1)(functools.partial(run, (theirs_ref, mine_ref)))


def split(x):
    high = x.astype(BF16)
    return high, (x - high.astype(F32)).astype(BF16)


def product(left, right):
    a, c = split(left)
    b, d = split(right)
    dot = functools.partial(jnp.dot, preferred_element_type=F32)
    return dot(a, b) + dot(a, d) + dot(c, b)


def terms_kernel(own_ref, other_ref, right_ref, out_ref, left, right, sems):
    copies = []
    for z in range(8):
        at = z % 4 * 2 + z // 4
        copies.append(
            [
                pltpu.make_async_copy(own_ref.at[at], left.at[z, 0], sems.at[z, 0]),
                pltpu.make_async_copy(other_ref.at[at], left.at[z, 1], sems.at[z, 1]),
                pltpu.make_async_copy(right_ref.at[z], right.at[z], sems.at[z, 2]),
            ]
        )
    for group in copies:
        for copy in group:
            copy.start()
    total = None
    for z, group in enumerate(copies):
        for copy in group:
            copy.wait()
        x = product(jnp.concatenate([left[z, 0], left[z, 1]], axis=1), right[z].reshape(256, 512))
        total = x if total is None else total + x
    out_ref[...] = total


def terms(limit, own, other, right):
    far = pl.BlockSpec(memory_space=pl.ANY)
    return pl.pallas_call(
        terms_kernel,
        in_specs=[far] * 3,
        out_specs=pl.BlockSpec(memory_space=pltpu.VMEM),
        out_shape=jax.ShapeDtypeStruct((256, 512), F32),
        scratch_shapes=[
            pltpu.VMEM((8, 2, 256, 128), F32),
            pltpu.VMEM((8, 2, 128, 512), F32),
            pltpu.SemaphoreType.DMA((8, 3)),
        ],
        compiler_params=params(limit),
        cost_estimate=pl.CostEstimate(flops=6 * 256 * 2048 * 512, bytes_accessed=6 << 20, transcendentals=0),
    )(own, other, right)


def finish_kernel(half, mine_ref, got_ref, out_ref):
    own = (groups((256, 128), 32) % 2) == half()
    for t in range(4):
        mine = mine_ref[:, 128 * t : 128 * t + 128]
        got = got_ref[:, 128 * t : 128 * t + 128]
        out_ref[:, 256 * t : 256 * t + 128] = jnp.where(own, mine, got)
        out_ref[:, 256 * t + 128 : 256 * t + 256] = pltpu.roll(jnp.where(own, got, mine), 96, 1)


def core_index():
    return lax.axis_index("c")


def half_index():
    return lax.rem(lax.axis_index("l"), 2)


def call(kernel, shape, *ops, cost=0):
    spec = pl.BlockSpec(memory_space=pltpu.VMEM)
    outs = len(shape) if isinstance(shape, list) else 0
    out = [jax.ShapeDtypeStruct(s, F32) for s in shape] if outs else jax.ShapeDtypeStruct(shape, F32)
    return pl.pallas_call(
        kernel,
        in_specs=[spec] * len(ops),
        out_specs=[spec] * outs if outs else spec,
        out_shape=out,
        compiler_params=params(),
        cost_estimate=pl.CostEstimate(flops=cost, bytes_accessed=1 << 20, transcendentals=0),
    )(*ops)


def after(x, *others):
    return lax.optimization_barrier((x, *others))[0]


def swap(x, axis, n):
    return lax.ppermute(x, axis, [(i, i ^ 1) for i in range(n)])


def shards(left, right):
    r = call(pack_right_kernel, (64, 16, 128), right)
    q = call(pack_left_kernel, (64, 16, 128), left)
    r = lax.all_to_all(r, ("h", "x", "c", "l"), 0, 0, tiled=True)
    r = call(functools.partial(unpack_right_kernel, core_index, half_index), (2, 4, 2, 16, 512), r)
    r = r.reshape(2, 128, 512)
    w = lax.all_gather(r, "z", axis=0, tiled=False)

    q = lax.all_to_all(after(q, r), ("z", "h", "l"), 0, 0, tiled=True)
    theirs, mine = call(functools.partial(unpack_left_kernel, half_index), [(4, 2, 256, 128)] * 2, q)
    own1 = lax.all_to_all(theirs, "x", 0, 0, tiled=True).reshape(8, 256, 128)
    own2 = lax.all_to_all(after(mine, own1), "x", 0, 0, tiled=True).reshape(8, 256, 128)
    other1 = swap(own1, "c", 2)

    theirs = terms(60, own1, other1, w)
    got = swap(theirs, "l", 4)
    other2 = swap(own2, "c", 2)
    mine = terms(20, own2, other2, w)
    return call(functools.partial(finish_kernel, half_index), (256, 1024), mine, got)


def solution(mesh):
    fine = Mesh(mesh.devices.reshape(8, 2, 4, 2, 4), ("z", "h", "x", "c", "l"))
    col = ("h", "x", "c")
    return jax.shard_map(
        shards,
        mesh=fine,
        in_specs=(P(("l",) + col, "z"), P(("l", "z"), col)),
        out_specs=P(("z", "l"), col),
        check_vma=False,
    )
```

```python
import functools

import jax
import jax.numpy as jnp
from jax import lax
from jax.experimental import pallas as pl
from jax.experimental.pallas import tpu as pltpu
from jax.sharding import Mesh, PartitionSpec as P

F32 = jnp.float32
BF16 = jnp.bfloat16
PLACE = ((0, 2, 1, 3), (1, 3, 2, 0))


def params(limit=8):
    return pltpu.CompilerParams(vmem_limit_bytes=limit * 1024 * 1024)


def groups(shape, width):
    return lax.broadcasted_iota(jnp.int32, shape, len(shape) - 1) // width


def pick(where, parts):
    out = parts[0]
    for g in range(1, len(parts)):
        out = jnp.where(where == g, parts[g], out)
    return out


def pack_right_kernel(x_ref, out_ref):
    g = groups((16, 128), 32)
    for hx in range(8):
        rolled = []
        for i in range(4):
            tile = x_ref[16 * i : 16 * i + 16, 128 * hx : 128 * hx + 128]
            rolled.append(pltpu.roll(tile, 32 * i, 1) if i else tile)
        for p in range(4):
            msg = pick(g, [rolled[(k - p) % 4] for k in range(4)])
            for a in range(2):
                out_ref[(2 * hx + p // 2) * 4 + 2 * a + p % 2] = msg


def unpack_right_kernel(core, half, in_ref, out_ref):
    g = groups((16, 128), 32)
    core, half = core(), half()
    p = 2 * core + half

    def run(place):
        for l in range(4):
            for t in range(4):
                rolled = []
                for m in range(4):
                    msg = in_ref[(4 * t + m) * 4 + l]
                    rolled.append(pltpu.roll(msg, 32 * place[m], 1) if place[m] else msg)
                for j in range(4):
                    order = [None] * 4
                    for m in range(4):
                        order[(j + place[m]) % 4] = rolled[m]
                    row = pick(g, order)
                    if j:
                        row = pltpu.roll(row, 32 * (4 - j), 1)
                    i = lax.rem(j - p + 4, 4)
                    s = i // 2
                    out_ref[lax.rem(s + core, 2), l, lax.rem(i, 2), :, 128 * t : 128 * t + 128] = row

    for h in range(2):
        pl.when(half == h)(functools.partial(run, PLACE[h]))


def pack_left_kernel(in_ref, out_ref):
    low = groups((16, 128), 64) == 0
    for z in range(8):
        top, bottom = in_ref[z, 0:16], in_ref[z, 16:32]
        first = jnp.where(low, top, pltpu.roll(bottom, 64, 1))
        second = jnp.where(low, pltpu.roll(top, 64, 1), bottom)
        for h in range(2):
            for b in range(2):
                out_ref[h * 4 + b, z] = first
                out_ref[h * 4 + 2 + b, z] = second


def unpack_left_kernel(half, in_ref, theirs_ref, mine_ref):
    low = groups((16, 128), 64) == 0

    def run(outs):
        for h in range(2):
            for t in range(4):
                rows = []
                for l in range(4):
                    even = in_ref[h * 4 + l, 2 * t]
                    odd = in_ref[h * 4 + l, 2 * t + 1]
                    rows.append(jnp.where(low, even, pltpu.roll(odd, 64, 1)))
                    rows.append(jnp.where(low, pltpu.roll(even, 64, 1), odd))
                block = jnp.concatenate(rows, axis=0).T
                out, rows = outs[t // 2], slice(t % 2 * 128, t % 2 * 128 + 128)
                if len(out.shape) == 3:
                    out[h, rows] = block
                else:
                    for d in range(4):
                        out[d, h, rows] = block

    half = half()
    pl.when(half == 0)(functools.partial(run, (mine_ref, theirs_ref)))
    pl.when(half == 1)(functools.partial(run, (theirs_ref, mine_ref)))


def split(x):
    high = x.astype(BF16)
    return high, (x - high.astype(F32)).astype(BF16)


def product(left, right):
    a, c = split(left)
    b, d = split(right)
    dot = functools.partial(jnp.dot, preferred_element_type=F32)
    return dot(a, b) + dot(a, d) + dot(c, b)


def terms_kernel(*refs):
    own_ref, *other_refs, right_ref, out_ref, left, right, sems = refs
    each = 4 // len(other_refs)
    copies = []
    for z in range(8):
        x, h = z % 4, z // 4
        group = [pltpu.make_async_copy(right_ref.at[z], right.at[z], sems.at[z, 2])]
        group.append(pltpu.make_async_copy(own_ref.at[x, h], left.at[z, 0], sems.at[z, 0]))
        group.append(pltpu.make_async_copy(other_refs[x // each].at[x % each, h], left.at[z, 1], sems.at[z, 1]))
        copies.append(group)
    for group in copies:
        for copy in group:
            copy.start()
    total = None
    for z, group in enumerate(copies):
        for copy in group:
            copy.wait()
        x = product(jnp.concatenate([left[z, 0], left[z, 1]], axis=1), right[z].reshape(256, 512))
        total = x if total is None else total + x
    out_ref[...] = total


def terms(limit, right, *left):
    far = pl.BlockSpec(memory_space=pl.ANY)
    return pl.pallas_call(
        terms_kernel,
        in_specs=[far] * (1 + len(left)),
        out_specs=pl.BlockSpec(memory_space=pltpu.VMEM),
        out_shape=jax.ShapeDtypeStruct((256, 512), F32),
        scratch_shapes=[
            pltpu.VMEM((8, 2, 256, 128), F32),
            pltpu.VMEM((8, 2, 128, 512), F32),
            pltpu.SemaphoreType.DMA((8, 3)),
        ],
        compiler_params=params(limit),
        cost_estimate=pl.CostEstimate(flops=6 * 256 * 2048 * 512, bytes_accessed=6 << 20, transcendentals=0),
    )(*left, right)


def finish_kernel(half, mine_ref, got_ref, out_ref):
    own = (groups((256, 128), 32) % 2) == half()
    for t in range(4):
        mine = mine_ref[:, 128 * t : 128 * t + 128]
        got = got_ref[:, 128 * t : 128 * t + 128]
        out_ref[:, 256 * t : 256 * t + 128] = jnp.where(own, mine, got)
        out_ref[:, 256 * t + 128 : 256 * t + 256] = pltpu.roll(jnp.where(own, got, mine), 96, 1)


def core_index():
    return lax.axis_index("c")


def half_index():
    return lax.rem(lax.axis_index("l"), 2)


def call(kernel, shape, *ops, cost=0):
    spec = pl.BlockSpec(memory_space=pltpu.VMEM)
    outs = len(shape) if isinstance(shape, list) else 0
    out = [jax.ShapeDtypeStruct(s, F32) for s in shape] if outs else jax.ShapeDtypeStruct(shape, F32)
    return pl.pallas_call(
        kernel,
        in_specs=[spec] * len(ops),
        out_specs=[spec] * outs if outs else spec,
        out_shape=out,
        compiler_params=params(),
        cost_estimate=pl.CostEstimate(flops=cost, bytes_accessed=1 << 20, transcendentals=0),
    )(*ops)


def after(x, *others):
    return lax.optimization_barrier((x, *others))[0]


def swap(x, axis, n):
    return lax.ppermute(x, axis, [(i, i ^ 1) for i in range(n)])


def shards(left, right):
    r = call(pack_right_kernel, (64, 16, 128), right)
    q = left.reshape(32, 8, 128).transpose(1, 0, 2)
    r = lax.all_to_all(r, ("h", "x", "c", "l"), 0, 0, tiled=True)
    r = call(functools.partial(unpack_right_kernel, core_index, half_index), (2, 4, 2, 16, 512), r)
    r = r.reshape(2, 128, 512)
    w = lax.all_gather(r, "z", axis=0, tiled=False)

    q = lax.all_to_all(after(q, r), "z", 0, 0, tiled=True)
    q = call(pack_left_kernel, (8, 8, 16, 128), q)
    q = lax.all_to_all(q, ("h", "l"), 0, 0, tiled=True)
    theirs, mine = call(functools.partial(unpack_left_kernel, half_index), [(4, 2, 256, 128)] * 2, q)
    own1 = lax.all_to_all(theirs, "x", 0, 0, tiled=True)
    own2 = lax.all_to_all(after(mine, own1), "x", 0, 0, tiled=True)

    theirs = terms(60, w, own1, *[swap(part, "c", 2) for part in jnp.split(own1, 2)])
    got = swap(theirs, "l", 4)
    own2 = after(own2, theirs)
    mine = terms(20, w, own2, swap(own2, "c", 2))
    return call(functools.partial(finish_kernel, half_index), (256, 1024), mine, got)


def solution(mesh):
    fine = Mesh(mesh.devices.reshape(8, 2, 4, 2, 4), ("z", "h", "x", "c", "l"))
    col = ("h", "x", "c")
    return jax.shard_map(
        shards,
        mesh=fine,
        in_specs=(P(("l",) + col, "z"), P(("l", "z"), col)),
        out_specs=P(("z", "l"), col),
        check_vma=False,
    )
```
